32 devices in a mesh: maps: 2 (over y), row: 4 (over z), col: 4 (over x, core).
Axes of the slice: x: 2, y: 2, z: 4, core: 2. Of those that a mesh axis runs over, the one named last changes fastest.
Arguments:
- tokens: bfloat16 [64, 512, 576], P(('maps', 'row'), 'col'), parts along dimension 0, may hold values from -6 to 6
- w_qkv: bfloat16 [576, 1728], replicated, may hold values from -0.25 to 0.25
- pool_kernel: bfloat16 [2, 9, 9, 72], replicated, may hold values from -0.625 to 0.625
- key_gain: float32 [72], replicated, may hold values from 1.5 to 80
- value_gain: float32 [72], replicated, may hold values from 0.5 to 2
- w_proj: bfloat16 [576, 576], replicated, may hold values from -0.25 to 0.25
- w_up: bfloat16 [576, 2304], replicated, may hold values from -0.25 to 0.25
- w_down: bfloat16 [2304, 576], replicated, may hold values from -0.125 to 0.125
Outputs:
- block_out: bfloat16 [64, 512, 576], P(('maps', 'row'), 'col'), parts along dimension 0
The draws below stay inside these ranges and needn't reach their ends.
There are 2 independent parts, one for each index of `maps`. The reference program is written for one: setup_inputs(seed, part) draws one part's arguments, and reference() takes and returns one part's arrays. A program takes and returns all parts, laid end to end along the dimension named above; an argument that names none is the same for every part. Nothing has to cross between parts.
All inputs are finite; a program needn't handle non-finite values.
Results may differ from the reference program's by a relative error of at most 0.0095.
The reference program's roundings to bfloat16 on the way (of `normed`, `qkv`, `pooled_kv`, `probs`, `attended`, `residual` and `hidden_act`) count: a program that leaves them out, or rounds other values in their place, can miss the bound.
Values may be sent and summed in bfloat16 or wider, within the bound.
A program may use at most 128 MiB of HBM per device.

```python
import math
import jax
import jax.numpy as jnp
from jax import lax

C = 576
HEADS = 8
FFN = 2304
HEAD_DIM = 72
STRIDE = 8
KERNEL = 9
H = 32
W = 512


def draw_key_gain(key, part):
    logs = jax.random.uniform(key, (HEAD_DIM,), jnp.float32, jnp.log(1.5), jnp.log(4.5))
    return jnp.exp(logs)


def block_levels(rng, extent, cuts, least, top_value):
    def one(axis_at, parts):
        draws = jax.random.uniform(jax.random.fold_in(jax.random.fold_in(rng, 6), axis_at), (parts,), jnp.float32, least / len(cuts), top_value / len(cuts))
        return jnp.repeat(jnp.exp(draws), extent[axis_at] // parts).reshape((-1,) + (1,) * (len(extent) - axis_at - 1))

    level = one(*cuts[0])
    for cut in cuts[1:]:
        level = level * one(*cut)
    return level


def noise(key, shape, scale, limit, cuts=(), dtype=jnp.bfloat16):
    level = block_levels(key, shape, cuts, -0.22, 0.18) if cuts else 1.0
    array = jax.random.normal(key, shape, jnp.float32) * scale * level
    return jnp.minimum(jnp.maximum(array, -limit), limit).astype(dtype)


def setup_inputs(seed: int = 0, part: int = 0) -> dict:
    key_list = jax.random.split(jax.random.key(seed), 9)
    part_keys = jax.random.split(jax.random.fold_in(key_list[8], part), 9)
    tokens = noise(part_keys[0], (H, W, C), 1.0, 6.0, ((0, 4), (1, 4)))
    w_qkv = noise(key_list[1], (C, 3 * C), C ** -0.5, 0.25)
    pool_kernel = noise(key_list[2], (2, KERNEL, KERNEL, HEAD_DIM), (KERNEL * KERNEL) ** -0.5, 0.625)
    key_gain = draw_key_gain(jax.random.fold_in(key_list[8], 71), part)
    value_gain = jnp.clip(jnp.exp(jax.random.uniform(key_list[4], (HEAD_DIM,), jnp.float32, math.log(0.5), math.log(2.0))), 0.5, 2.0)
    w_proj = noise(key_list[5], (C, C), C ** -0.5, 0.25)
    w_up = noise(key_list[6], (C, FFN), C ** -0.5, 0.25)
    w_down = noise(key_list[7], (FFN, C), FFN ** -0.5, 0.125)
    return dict(tokens=tokens, w_qkv=w_qkv, pool_kernel=pool_kernel, key_gain=key_gain, value_gain=value_gain, w_proj=w_proj, w_up=w_up, w_down=w_down)


EPS = 1e-06

def layer_norm(values):
    mean = lax.optimization_barrier(jnp.mean(values, axis=-1, keepdims=True))
    centred = values - mean
    spread = lax.optimization_barrier(jnp.mean(centred * centred, axis=-1, keepdims=True))
    return centred * lax.rsqrt(spread + EPS)

def pool(framed, kernel, heads, stride, pad):
    head_dim = kernel.shape[-1]
    span = kernel.shape[1]
    channels = 2 * head_dim * heads
    full = jnp.concatenate([jnp.tile(kernel[0], (1, 1, heads)), jnp.tile(kernel[1], (1, 1, heads))], axis=-1)
    full = full.reshape(span, span, 1, channels)
    result = lax.conv_general_dilated(framed[None], full, (stride, stride), ((pad, pad), (pad, pad)), dimension_numbers=('NHWC', 'HWIO', 'NHWC'), feature_group_count=channels, preferred_element_type=jnp.float32)
    return result[0]

def norm_pooled(pooled, key_gain, value_gain, heads):
    count = pooled.shape[0]
    head_dim = key_gain.shape[0]
    split = pooled.reshape(count, 2, heads, head_dim)
    gains = jnp.stack([key_gain, value_gain]).reshape(1, 2, 1, head_dim)
    return (layer_norm(split) * gains).reshape(count, 2 * heads * head_dim).astype(jnp.bfloat16)

def finish_block(query_block, token_block, keys, values, w_proj, w_up, w_down, heads):
    count, width = query_block.shape
    head_dim = width // heads
    query = query_block.reshape(count, heads, head_dim)
    scores = jnp.einsum('qhd,khd->hqk', query.astype(jnp.float32), keys.astype(jnp.float32)) * head_dim ** (-0.5)
    top = lax.optimization_barrier(jnp.max(scores, axis=-1, keepdims=True))
    weights = jnp.exp(scores - top)
    total = lax.optimization_barrier(jnp.sum(weights, axis=-1))
    probs = weights.astype(jnp.bfloat16)
    mixed = jnp.einsum('hqk,khd->qhd', probs.astype(jnp.float32), values.astype(jnp.float32))
    mixed = mixed / jnp.transpose(total)[:, :, None] + query.astype(jnp.float32)
    attended = mixed.reshape(count, width).astype(jnp.bfloat16)
    residual = (token_block.astype(jnp.float32) + jnp.dot(attended, w_proj, preferred_element_type=jnp.float32)).astype(jnp.bfloat16)
    renormed = layer_norm(residual.astype(jnp.float32)).astype(jnp.bfloat16)
    hidden_act = jax.nn.gelu(jnp.dot(renormed, w_up, preferred_element_type=jnp.float32), approximate=False).astype(jnp.bfloat16)
    return (residual.astype(jnp.float32) + jnp.dot(hidden_act, w_down, preferred_element_type=jnp.float32)).astype(jnp.bfloat16)

def reference(tokens, w_qkv, pool_kernel, key_gain, value_gain, w_proj, w_up, w_down):
    rows, cols, width = tokens.shape
    heads = HEADS
    head_dim = width // heads
    count = rows * cols
    block = min(count, 4096)
    flat = tokens.reshape(count // block, block, width)

    def project(token_block):
        normed = layer_norm(token_block.astype(jnp.float32)).astype(jnp.bfloat16)
        return jnp.dot(normed, w_qkv, preferred_element_type=jnp.float32).astype(jnp.bfloat16)
    qkv = lax.map(project, flat)
    query = qkv[:, :, :width]
    keyval = qkv[:, :, width:].reshape(rows, cols, 2 * width)
    pooled = pool(keyval, pool_kernel, heads, STRIDE, KERNEL // 2)
    pooled = pooled.reshape(-1, 2 * width)
    pooled_kv = norm_pooled(pooled, key_gain, value_gain, heads)
    keys = pooled_kv[:, :width].reshape(-1, heads, head_dim)
    values = pooled_kv[:, width:].reshape(-1, heads, head_dim)

    def finish(pair):
        return finish_block(pair[0], pair[1], keys, values, w_proj, w_up, w_down, heads)
    result = lax.map(finish, (query, flat))
    return result.reshape(rows, cols, width)
```

```python
import functools
import math

import jax
import jax.numpy as jnp
from jax import lax
from jax.experimental import pallas as pl
from jax.experimental.pallas import tpu as pltpu
from jax.sharding import PartitionSpec as P

HEADS = 8
STRIDE = 8
EPS = 1e-06
LANES = 128
MESH = pl.DeviceIdType.MESH
F32 = jnp.float32
BF16 = jnp.bfloat16


def layer_norm(values):
    mean = jnp.mean(values, axis=-1, keepdims=True)
    centred = values - mean
    spread = jnp.mean(centred * centred, axis=-1, keepdims=True)
    return centred * lax.rsqrt(spread + EPS)


def spread_matrix(head_dim, width, heads, shift, dtype):
    feature = lax.broadcasted_iota(jnp.int32, (head_dim, width), 0)
    lane = lax.broadcasted_iota(jnp.int32, (head_dim, width), 1) - shift
    hit = lane == feature
    for head in range(1, heads):
        hit = hit | (lane == feature + head * head_dim)
    return jnp.where(hit, 1.0, 0.0).astype(dtype)


def pooled_keys_kernel(
    rows_n, cols_n, heads,
    tokens_ref, w_ref, pool_ref, key_gain_ref, value_gain_ref,
    q_ref, gathered_ref,
    normed, keyval, taps, own, blocks,
    down_out, down_in, diag_out, diag_in, right_out, right_in,
    halo_send, halo_recv, send_sem, recv_sem,
):
    count, width = tokens_ref.shape
    head_dim = width // heads
    cols = count // STRIDE
    groups = cols // STRIDE
    span = pool_ref.shape[1]
    reach = span // 2
    aligned = width // LANES * LANES
    shift = width - aligned
    wide = shift + 2 * width
    row, col = lax.axis_index("row"), lax.axis_index("col")
    has_up, has_down = row > 0, row < rows_n - 1
    has_left, has_right = col > 0, col < cols_n - 1
    to_diag = jnp.logical_and(has_down, has_right)
    from_diag = jnp.logical_and(has_up, has_left)

    barrier = pltpu.get_barrier_semaphore()
    for step in range(1, rows_n):
        pl.semaphore_signal(
            barrier, inc=1, device_id={"row": lax.rem(row + step, rows_n)}, device_id_type=MESH)
    for step in range(1, cols_n):
        pl.semaphore_signal(
            barrier, inc=1, device_id={"col": lax.rem(col + step, cols_n)}, device_id_type=MESH)

    @pl.when(to_diag)
    def _():
        pl.semaphore_signal(
            barrier, inc=1, device_id={"row": row + 1, "col": col + 1}, device_id_type=MESH)

    @pl.when(from_diag)
    def _():
        pl.semaphore_signal(
            barrier, inc=1, device_id={"row": row - 1, "col": col - 1}, device_id_type=MESH)

    key_spread = spread_matrix(head_dim, shift + width, heads, shift, BF16)
    value_spread = spread_matrix(head_dim, width, heads, 0, BF16)
    for a in range(span):
        line = jnp.concatenate(
            [
                jnp.dot(pool_ref[0, a], key_spread, preferred_element_type=F32),
                jnp.dot(pool_ref[1, a], value_spread, preferred_element_type=F32),
            ],
            axis=-1,
        )
        below = jnp.zeros((STRIDE - reach - 1, wide), F32)
        above = jnp.zeros((STRIDE - reach, wide), F32)
        taps[0, a] = jnp.concatenate([line[reach:], below], axis=0)
        taps[1, a] = jnp.concatenate([above, line[:reach]], axis=0)

    def project(first, last):
        for at in range(first, last):
            line = pl.ds(at * cols, cols)
            normed[line, :] = layer_norm(tokens_ref[line, :].astype(F32)).astype(BF16)
        part = pl.ds(first * cols, (last - first) * cols)
        keyval[part, :] = jnp.dot(
            normed[part, :], w_ref[:, aligned:], preferred_element_type=F32).astype(BF16)

    def pool(first, last, offset, here, beyond):
        for start in range(0, wide, LANES):
            lanes = slice(start, min(start + LANES, wide))
            low, high = None, None
            for at in range(first, last):
                values = keyval[at * cols:(at + 1) * cols, lanes].astype(F32)
                values = values.reshape(groups, STRIDE, values.shape[-1])
                one = values * taps[0, at + offset, :, lanes][None]
                two = values * taps[1, at + offset, :, lanes][None]
                low = one if low is None else low + one
                high = two if high is None else high + two
            moved = jnp.concatenate([jnp.zeros_like(high[:1]), high[:-1]], axis=0)
            here[:, lanes] = jnp.sum(low + moved, axis=1)
            beyond[:, lanes] = jnp.sum(high[-1], axis=0, keepdims=True)

    def halo(at, source, target, device):
        return pltpu.make_async_remote_copy(
            src_ref=source, dst_ref=target, send_sem=halo_send.at[at], recv_sem=halo_recv.at[at],
            device_id=device, device_id_type=MESH)

    down = halo(0, down_out, down_in, {"row": lax.rem(row + 1, rows_n)})
    diag = halo(1, diag_out, diag_in,
                {"row": lax.rem(row + 1, rows_n), "col": lax.rem(col + 1, cols_n)})
    right = halo(2, right_out, right_in, {"col": lax.rem(col + 1, cols_n)})

    project(reach, STRIDE)
    pool(reach, STRIDE, -reach, down_out, diag_out)
    pl.semaphore_wait(
        barrier, rows_n - 1 + cols_n - 1 + to_diag.astype(jnp.int32) + from_diag.astype(jnp.int32))
    pl.when(has_down)(down.start)
    pl.when(to_diag)(diag.start)
    project(0, reach)
    pool(0, reach + 1, reach, own, right_out)
    pl.when(has_right)(right.start)

    q_ref[:, :aligned] = jnp.dot(
        normed[...], w_ref[:, :aligned], preferred_element_type=F32).astype(BF16)
    q_ref[:, aligned:] = keyval[:, :shift]

    @pl.when(jnp.logical_not(has_up))
    def _():
        down_in[...] = jnp.zeros_like(down_in)

    @pl.when(jnp.logical_not(from_diag))
    def _():
        diag_in[...] = jnp.zeros_like(diag_in)

    @pl.when(jnp.logical_not(has_left))
    def _():
        right_in[...] = jnp.zeros_like(right_in)

    pl.when(has_up)(down.wait_recv)
    pl.when(from_diag)(diag.wait_recv)
    pl.when(has_left)(right.wait_recv)

    total = own[...] + down_in[...]
    first_row = lax.broadcasted_iota(jnp.int32, total.shape, 0) == 0
    total = total + jnp.where(first_row, right_in[...] + diag_in[...], 0.0)
    lane = lax.broadcasted_iota(jnp.int32, (1, wide), 1) - shift
    masks = [
        (lane >= at * head_dim) & (lane < (at + 1) * head_dim) for at in range(2 * heads)
    ]

    def head_mean(values):
        result = jnp.zeros_like(values)
        for mask in masks:
            mean = jnp.sum(jnp.where(mask, values, 0.0), axis=-1, keepdims=True) / head_dim
            result = jnp.where(mask, mean, result)
        return result

    def spread_gain(gain_ref, matrix):
        gain = jnp.broadcast_to(gain_ref[...], (8, head_dim))
        return jnp.dot(gain, matrix.astype(F32), precision=lax.Precision.HIGHEST,
                       preferred_element_type=F32)[:1]

    gains = jnp.concatenate(
        [spread_gain(key_gain_ref, key_spread), spread_gain(value_gain_ref, value_spread)], axis=-1)
    centred = total - head_mean(total)
    scaled = centred * lax.rsqrt(head_mean(centred * centred) + EPS) * gains
    me = row * cols_n + col
    blocks[me] = scaled[:, shift:].astype(BF16)

    sends = []

    def send(block, device):
        copy = pltpu.make_async_remote_copy(
            src_ref=blocks.at[block], dst_ref=blocks.at[block],
            send_sem=send_sem.at[len(sends)], recv_sem=recv_sem.at[block],
            device_id=device, device_id_type=MESH)
        copy.start()
        sends.append(copy)

    def arrive(block):
        pltpu.make_async_remote_copy(
            src_ref=blocks.at[block], dst_ref=blocks.at[block],
            send_sem=send_sem.at[0], recv_sem=recv_sem.at[block],
            device_id={"col": lax.rem(col + 1, cols_n)}, device_id_type=MESH).wait_recv()

    def flipped(bit):
        return col + bit - 2 * bit * lax.rem(col // bit, 2)

    bits = []
    bit = cols_n // 2
    while bit >= 1:
        bits.append(bit)
        bit //= 2
    order = [0]
    for step in range(1, rows_n // 2 + 1):
        order += [step] if 2 * step == rows_n else [step, rows_n - step]
    for step in reversed(order[1:]):
        send(me, {"row": lax.rem(row + step, rows_n)})
    have = [col]
    for level in range(len(bits) + 1):
        fresh = have if level == 0 else have[len(have) // 2:]
        for at in fresh:
            for step in order:
                block = lax.rem(row + step, rows_n) * cols_n + at
                if not (level == 0 and step == 0):
                    arrive(block)
                for bit in bits[level:]:
                    send(block, {"col": flipped(bit)})
        if level < len(bits):
            bit = bits[level]
            have = have + [at + bit - 2 * bit * lax.rem(at // bit, 2) for at in have]
    gathered_ref[...] = blocks[...]
    for copy in sends:
        copy.wait_send()
    pl.when(has_down)(down.wait_send)
    pl.when(to_diag)(diag.wait_send)
    pl.when(has_right)(right.wait_send)


def pooled_keys(tokens, w_qkv, pool_kernel, key_gain, value_gain, rows_n, cols_n):
    count, width = tokens.shape
    groups = count // STRIDE // STRIDE
    span = pool_kernel.shape[1]
    shift = width % LANES
    wide = shift + 2 * width
    spaces = rows_n * cols_n
    bits = cols_n.bit_length() - 1
    sends = rows_n - 1 + rows_n * (cols_n - 1)
    vmem = pl.BlockSpec(memory_space=pltpu.VMEM)
    return pl.pallas_call(
        functools.partial(pooled_keys_kernel, rows_n, cols_n, HEADS),
        out_shape=[
            jax.ShapeDtypeStruct((count, width), BF16),
            jax.ShapeDtypeStruct((spaces, groups, 2 * width), BF16),
        ],
        in_specs=[vmem] * 5,
        out_specs=[vmem] * 2,
        scratch_shapes=[
            pltpu.VMEM((count, width), BF16),
            pltpu.VMEM((count, wide), BF16),
            pltpu.VMEM((2, span, STRIDE, wide), F32),
            pltpu.VMEM((groups, wide), F32),
            pltpu.VMEM((spaces, groups, 2 * width), BF16),
            pltpu.VMEM((groups, wide), F32),
            pltpu.VMEM((groups, wide), F32),
            pltpu.VMEM((1, wide), F32),
            pltpu.VMEM((1, wide), F32),
            pltpu.VMEM((1, wide), F32),
            pltpu.VMEM((1, wide), F32),
            pltpu.SemaphoreType.DMA((3,)),
            pltpu.SemaphoreType.DMA((3,)),
            pltpu.SemaphoreType.DMA((sends,)),
            pltpu.SemaphoreType.DMA((spaces,)),
        ],
        compiler_params=pltpu.CompilerParams(
            collective_id=0, has_side_effects=True, vmem_limit_bytes=36 * 2**20),
        cost_estimate=pl.CostEstimate(
            flops=2 * count * width * 3 * width, bytes_accessed=6 * 2**20, transcendentals=0),
        name="pooled_keys",
    )(tokens, w_qkv, pool_kernel, key_gain.reshape(1, -1), value_gain.reshape(1, -1))


def windows(width, heads):
    head_dim = width // heads
    result = []
    for head in range(0, heads, 2):
        start = head * head_dim // LANES * LANES
        stop = min(-(-(head + 2) * head_dim // LANES) * LANES, width)
        result.append((start, stop, head * head_dim - start))
    return result


def finish_kernel(heads, q_ref, tokens_ref, pooled_ref, w_proj_ref, w_up_ref, w_down_ref,
                  out_ref, keys, values):
    rows, width = q_ref.shape
    head_dim = width // heads
    spots = pooled_ref.shape[0]
    places = windows(width, heads)

    @pl.when(pl.program_id(0) == 0)
    def _():
        all_keys = pooled_ref[:, :width]
        all_values = pooled_ref[:, width:]
        for pair, (start, stop, at) in enumerate(places):
            lane = lax.broadcasted_iota(jnp.int32, (spots, stop - start), 1)
            for side in range(2):
                first = at + side * head_dim
                mask = (lane >= first) & (lane < first + head_dim)
                spot = pl.ds(side * spots, spots)
                keys[pair, spot, :stop - start] = jnp.where(
                    mask, all_keys[:, start:stop].astype(F32), 0.0).astype(BF16)
                values[pair, spot, :stop - start] = jnp.where(
                    mask, all_values[:, start:stop].astype(F32), 0.0).astype(BF16)

    factor = head_dim ** -0.5 * math.log2(math.e)
    tiles = [None] * (-(-width // LANES))
    for pair, (start, stop, at) in enumerate(places):
        size = stop - start
        scores = lax.dot_general(
            q_ref[:, start:stop], keys[pair, :, :size], (((1,), (1,)), ((), ())),
            preferred_element_type=F32)
        probs, scales = [], []
        for side in range(2):
            part = scores[:, side * spots:(side + 1) * spots]
            top = jnp.max(part, axis=-1, keepdims=True)
            weights = jnp.exp2((part - top) * factor)
            scales.append(1.0 / jnp.sum(weights, axis=-1, keepdims=True))
            probs.append(weights.astype(BF16))
        mixed = jnp.dot(jnp.concatenate(probs, axis=-1), values[pair, :, :size],
                        preferred_element_type=F32)
        lane = lax.broadcasted_iota(jnp.int32, (1, size), 1)
        mixed = mixed * jnp.where(lane < at + head_dim, scales[0], scales[1])
        for tile in range(0, size, LANES):
            piece = mixed[:, tile:tile + LANES]
            index = (start + tile) // LANES
            tiles[index] = piece if tiles[index] is None else tiles[index] + piece
    attended = (jnp.concatenate(tiles, axis=-1) + q_ref[...].astype(F32)).astype(BF16)
    residual = (
        tokens_ref[...].astype(F32)
        + jnp.dot(attended, w_proj_ref[...], preferred_element_type=F32)
    ).astype(BF16)
    residual = residual.astype(F32)
    renormed = layer_norm(residual).astype(BF16)
    ffn = w_up_ref.shape[1]
    chunk = math.gcd(ffn, 768)
    total = residual
    for start in range(0, ffn, chunk):
        hidden = jnp.dot(renormed, w_up_ref[:, start:start + chunk], preferred_element_type=F32)
        active = (hidden * (0.5 + 0.5 * lax.erf(hidden * (0.5 ** 0.5)))).astype(BF16)
        total = total + jnp.dot(active, w_down_ref[start:start + chunk, :],
                                preferred_element_type=F32)
    out_ref[...] = total.astype(BF16)


def finish(query, tokens, pooled, w_proj, w_up, w_down):
    count, width = query.shape
    spots = pooled.shape[0]
    rows = math.gcd(count, 256 if spots <= 512 else 128)
    block = pl.BlockSpec((rows, width), lambda i: (i, 0))
    vmem = pl.BlockSpec(memory_space=pltpu.VMEM)
    places = windows(width, HEADS)
    size = max(stop - start for start, stop, _ in places)
    ffn = w_up.shape[1]
    return pl.pallas_call(
        functools.partial(finish_kernel, HEADS),
        grid=(count // rows,),
        out_shape=jax.ShapeDtypeStruct((count, width), BF16),
        in_specs=[block, block, vmem, vmem, vmem, vmem],
        out_specs=block,
        scratch_shapes=[
            pltpu.VMEM((len(places), 2 * spots, size), BF16),
            pltpu.VMEM((len(places), 2 * spots, size), BF16),
        ],
        compiler_params=pltpu.CompilerParams(vmem_limit_bytes=52 * 2**20),
        cost_estimate=pl.CostEstimate(
            flops=2 * count * width * (width + 2 * ffn + 2 * spots),
            bytes_accessed=10 * 2**20, transcendentals=count * (ffn + HEADS * spots)),
        name="finish",
    )(query, tokens, pooled, w_proj, w_up, w_down)


def per_device(rows_n, cols_n, tokens, w_qkv, pool_kernel, key_gain, value_gain, w_proj, w_up,
               w_down):
    rows, cols, width = tokens.shape
    flat = tokens.reshape(rows * cols, width)
    query, pooled = pooled_keys(flat, w_qkv, pool_kernel, key_gain, value_gain, rows_n, cols_n)
    result = finish(query, flat, pooled.reshape(-1, 2 * width), w_proj, w_up, w_down)
    return result.reshape(rows, cols, width)


def solution(mesh):
    in_specs = (P(("maps", "row"), "col", None), P(), P(), P(), P(), P(), P(), P())
    out_specs = P(("maps", "row"), "col", None)
    body = functools.partial(per_device, mesh.shape["row"], mesh.shape["col"])
    return jax.shard_map(
        body, mesh=mesh, in_specs=in_specs, out_specs=out_specs, check_vma=False
    )
```

```python
import functools
import math

import jax
import jax.numpy as jnp
from jax import lax
from jax.experimental import pallas as pl
from jax.experimental.pallas import tpu as pltpu
from jax.sharding import PartitionSpec as P

HEADS = 8
STRIDE = 8
EPS = 1e-06
LANES = 128
MESH = pl.DeviceIdType.MESH
F32 = jnp.float32
BF16 = jnp.bfloat16


def layer_norm(values, axis):
    mean = jnp.mean(values, axis=axis, keepdims=True)
    centred = values - mean
    spread = jnp.mean(centred * centred, axis=axis, keepdims=True)
    return centred * lax.rsqrt(spread + EPS)


def spread_matrix(head_dim, width, heads, shift, dtype):
    feature = lax.broadcasted_iota(jnp.int32, (head_dim, width), 0)
    lane = lax.broadcasted_iota(jnp.int32, (head_dim, width), 1) - shift
    hit = lane == feature
    for head in range(1, heads):
        hit = hit | (lane == feature + head * head_dim)
    return jnp.where(hit, 1.0, 0.0).astype(dtype)


def pooled_keys_kernel(
    rows_n, cols_n, heads,
    tokens_ref, w_ref, pool_ref, key_gain_ref, value_gain_ref,
    q_ref, gathered_ref,
    normed, keyval, taps, own, blocks,
    down_out, down_in, diag_out, diag_in, right_out, right_in,
    halo_send, halo_recv, send_sem, recv_sem,
):
    _, width, cols = tokens_ref.shape
    head_dim = width // heads
    groups = cols // STRIDE
    span = pool_ref.shape[0]
    reach = span // 2
    aligned = width // LANES * LANES
    shift = width - aligned
    wide = shift + 2 * width
    row, col = lax.axis_index("row"), lax.axis_index("col")
    has_up, has_down = row > 0, row < rows_n - 1
    has_left, has_right = col > 0, col < cols_n - 1
    to_diag = jnp.logical_and(has_down, has_right)
    from_diag = jnp.logical_and(has_up, has_left)

    barrier = pltpu.get_barrier_semaphore()
    for step in range(1, rows_n):
        pl.semaphore_signal(
            barrier, inc=1, device_id={"row": lax.rem(row + step, rows_n)}, device_id_type=MESH)
    for step in range(1, cols_n):
        pl.semaphore_signal(
            barrier, inc=1, device_id={"col": lax.rem(col + step, cols_n)}, device_id_type=MESH)

    @pl.when(to_diag)
    def _():
        pl.semaphore_signal(
            barrier, inc=1, device_id={"row": row + 1, "col": col + 1}, device_id_type=MESH)

    @pl.when(from_diag)
    def _():
        pl.semaphore_signal(
            barrier, inc=1, device_id={"row": row - 1, "col": col - 1}, device_id_type=MESH)

    key_spread = spread_matrix(head_dim, shift + width, heads, shift, BF16)
    value_spread = spread_matrix(head_dim, width, heads, 0, BF16)
    def spread_taps(side, matrix):
        room = jnp.zeros((16 - span, head_dim), F32)
        lines = []
        for a in range(span):
            lines += [pool_ref[a].astype(F32)[:, side, :], room]
        lines = jnp.concatenate(lines, axis=0).astype(BF16)
        return jnp.dot(lines, matrix, preferred_element_type=F32)

    spread = jnp.concatenate([spread_taps(0, key_spread), spread_taps(1, value_spread)], axis=-1)
    for a in range(span):
        line = spread[16 * a:16 * a + span]
        below = jnp.zeros((STRIDE - reach - 1, wide), F32)
        above = jnp.zeros((STRIDE - reach, wide), F32)
        taps[0, a] = jnp.concatenate([line[reach:], below], axis=0)
        taps[1, a] = jnp.concatenate([above, line[:reach]], axis=0)

    def project(first, last):
        for at in range(first, last):
            line = pl.ds(at * cols, cols)
            normed[line, :] = jnp.transpose(
                layer_norm(tokens_ref[at].astype(F32), 0).astype(BF16))
        part = pl.ds(first * cols, (last - first) * cols)
        keyval[part, :] = jnp.dot(
            normed[part, :], w_ref[:, aligned:], preferred_element_type=F32).astype(BF16)

    def pool(first, last, offset, here, beyond):
        for start in range(0, wide, LANES):
            lanes = slice(start, min(start + LANES, wide))
            low, high = None, None
            for at in range(first, last):
                values = keyval[at * cols:(at + 1) * cols, lanes].astype(F32)
                values = values.reshape(groups, STRIDE, values.shape[-1])
                one = values * taps[0, at + offset, :, lanes][None]
                two = values * taps[1, at + offset, :, lanes][None]
                low = one if low is None else low + one
                high = two if high is None else high + two
            moved = jnp.concatenate([jnp.zeros_like(high[:1]), high[:-1]], axis=0)
            here[:, lanes] = jnp.sum(low + moved, axis=1)
            beyond[:, lanes] = jnp.sum(high[-1], axis=0, keepdims=True)

    def halo(at, source, target, device):
        return pltpu.make_async_remote_copy(
            src_ref=source, dst_ref=target, send_sem=halo_send.at[at], recv_sem=halo_recv.at[at],
            device_id=device, device_id_type=MESH)

    down = halo(0, down_out, down_in, {"row": lax.rem(row + 1, rows_n)})
    diag = halo(1, diag_out, diag_in,
                {"row": lax.rem(row + 1, rows_n), "col": lax.rem(col + 1, cols_n)})
    right = halo(2, right_out, right_in, {"col": lax.rem(col + 1, cols_n)})

    project(reach, STRIDE)
    pool(reach, STRIDE, -reach, down_out, diag_out)
    pl.semaphore_wait(
        barrier, rows_n - 1 + cols_n - 1 + to_diag.astype(jnp.int32) + from_diag.astype(jnp.int32))
    pl.when(has_down)(down.start)
    pl.when(to_diag)(diag.start)
    project(0, reach)
    pool(0, reach + 1, reach, own, right_out)
    pl.when(has_right)(right.start)

    q_ref[:, :aligned] = jnp.dot(
        normed[...], w_ref[:, :aligned], preferred_element_type=F32).astype(BF16)
    q_ref[:, aligned:] = keyval[:, :shift]

    @pl.when(jnp.logical_not(has_up))
    def _():
        down_in[...] = jnp.zeros_like(down_in)

    @pl.when(jnp.logical_not(from_diag))
    def _():
        diag_in[...] = jnp.zeros_like(diag_in)

    @pl.when(jnp.logical_not(has_left))
    def _():
        right_in[...] = jnp.zeros_like(right_in)

    pl.when(has_up)(down.wait_recv)
    pl.when(from_diag)(diag.wait_recv)
    pl.when(has_left)(right.wait_recv)

    total = own[...] + down_in[...]
    first_row = lax.broadcasted_iota(jnp.int32, total.shape, 0) == 0
    total = total + jnp.where(first_row, right_in[...] + diag_in[...], 0.0)
    lane = lax.broadcasted_iota(jnp.int32, (1, wide), 1) - shift
    masks = [
        (lane >= at * head_dim) & (lane < (at + 1) * head_dim) for at in range(2 * heads)
    ]

    def head_mean(values):
        result = jnp.zeros_like(values)
        for mask in masks:
            mean = jnp.sum(jnp.where(mask, values, 0.0), axis=-1, keepdims=True) / head_dim
            result = jnp.where(mask, mean, result)
        return result

    def spread_gain(gain_ref, matrix):
        gain = jnp.broadcast_to(gain_ref[...], (8, head_dim))
        return jnp.dot(gain, matrix.astype(F32), precision=lax.Precision.HIGHEST,
                       preferred_element_type=F32)[:1]

    gains = jnp.concatenate(
        [spread_gain(key_gain_ref, key_spread), spread_gain(value_gain_ref, value_spread)], axis=-1)
    centred = total - head_mean(total)
    scaled = centred * lax.rsqrt(head_mean(centred * centred) + EPS) * gains
    me = row * cols_n + col
    blocks[me] = scaled[:, shift:].astype(BF16)

    sends = []

    def send(block, device):
        copy = pltpu.make_async_remote_copy(
            src_ref=blocks.at[block], dst_ref=blocks.at[block],
            send_sem=send_sem.at[len(sends)], recv_sem=recv_sem.at[block],
            device_id=device, device_id_type=MESH)
        copy.start()
        sends.append(copy)

    def arrive(block):
        pltpu.make_async_remote_copy(
            src_ref=blocks.at[block], dst_ref=blocks.at[block],
            send_sem=send_sem.at[0], recv_sem=recv_sem.at[block],
            device_id={"col": lax.rem(col + 1, cols_n)}, device_id_type=MESH).wait_recv()

    def flipped(bit):
        return col + bit - 2 * bit * lax.rem(col // bit, 2)

    bits = []
    bit = cols_n // 2
    while bit >= 1:
        bits.append(bit)
        bit //= 2
    order = [0]
    for step in range(1, rows_n // 2 + 1):
        order += [step] if 2 * step == rows_n else [step, rows_n - step]
    for step in reversed(order[1:]):
        send(me, {"row": lax.rem(row + step, rows_n)})
    have = [col]
    for level in range(len(bits) + 1):
        fresh = have if level == 0 else have[len(have) // 2:]
        for at in fresh:
            for step in order:
                block = lax.rem(row + step, rows_n) * cols_n + at
                if not (level == 0 and step == 0):
                    arrive(block)
                for bit in bits[level:]:
                    send(block, {"col": flipped(bit)})
        if level < len(bits):
            bit = bits[level]
            have = have + [at + bit - 2 * bit * lax.rem(at // bit, 2) for at in have]
    gathered_ref[...] = blocks[...]
    for copy in sends:
        copy.wait_send()
    pl.when(has_down)(down.wait_send)
    pl.when(to_diag)(diag.wait_send)
    pl.when(has_right)(right.wait_send)


def pooled_keys(tokens, w_qkv, pool_kernel, key_gain, value_gain, rows_n, cols_n):
    rows, width, cols = tokens.shape
    count = rows * cols
    groups = cols // STRIDE
    span = pool_kernel.shape[0]
    shift = width % LANES
    wide = shift + 2 * width
    spaces = rows_n * cols_n
    sends = rows_n - 1 + rows_n * (cols_n - 1)
    vmem = pl.BlockSpec(memory_space=pltpu.VMEM)
    return pl.pallas_call(
        functools.partial(pooled_keys_kernel, rows_n, cols_n, HEADS),
        out_shape=[
            jax.ShapeDtypeStruct((count, width), BF16),
            jax.ShapeDtypeStruct((spaces, groups, 2 * width), BF16),
        ],
        in_specs=[vmem] * 5,
        out_specs=[vmem] * 2,
        scratch_shapes=[
            pltpu.VMEM((count, width), BF16),
            pltpu.VMEM((count, wide), BF16),
            pltpu.VMEM((2, span, STRIDE, wide), F32),
            pltpu.VMEM((groups, wide), F32),
            pltpu.VMEM((spaces, groups, 2 * width), BF16),
            pltpu.VMEM((groups, wide), F32),
            pltpu.VMEM((groups, wide), F32),
            pltpu.VMEM((1, wide), F32),
            pltpu.VMEM((1, wide), F32),
            pltpu.VMEM((1, wide), F32),
            pltpu.VMEM((1, wide), F32),
            pltpu.SemaphoreType.DMA((3,)),
            pltpu.SemaphoreType.DMA((3,)),
            pltpu.SemaphoreType.DMA((sends,)),
            pltpu.SemaphoreType.DMA((spaces,)),
        ],
        compiler_params=pltpu.CompilerParams(
            collective_id=0, has_side_effects=True, vmem_limit_bytes=(20 if spaces <= 16 else 40) * 2**20),
        cost_estimate=pl.CostEstimate(
            flops=2 * count * width * 3 * width, bytes_accessed=6 * 2**20, transcendentals=0),
        name="pooled_keys",
    )(tokens, w_qkv, pool_kernel, key_gain.reshape(1, -1), value_gain.reshape(1, -1))


def windows(width, heads):
    head_dim = width // heads
    result = []
    for head in range(0, heads, 2):
        start = head * head_dim // LANES * LANES
        stop = min(-(-(head + 2) * head_dim // LANES) * LANES, width)
        result.append((start, stop, head * head_dim - start))
    return result


def gelu(x):
    size = jnp.abs(x)
    t = pl.reciprocal(1.0 + (0.3275911 * 0.5 ** 0.5) * size, approx=False)
    tail = 0.5 * 1.061405429
    for term in (-1.453152027, 1.421413741, -0.284496736, 0.254829592):
        tail = tail * t + 0.5 * term
    tail = tail * t * jnp.exp2(x * x * (-0.5 * math.log2(math.e)))
    return jnp.maximum(x, 0.0) - size * tail


def finish_kernel(heads, q_ref, tokens_ref, pooled_ref, w_proj_ref, w_up_ref, w_down_ref,
                  out_ref, keys, values):
    rows, width = q_ref.shape
    head_dim = width // heads
    spots = pooled_ref.shape[0]
    places = windows(width, heads)

    @pl.when(pl.program_id(0) == 0)
    def _():
        all_keys = pooled_ref[:, :width]
        all_values = pooled_ref[:, width:]
        for pair, (start, stop, at) in enumerate(places):
            lane = lax.broadcasted_iota(jnp.int32, (spots, stop - start), 1)
            for side in range(2):
                first = at + side * head_dim
                mask = (lane >= first) & (lane < first + head_dim)
                spot = pl.ds(side * spots, spots)
                keys[pair, spot, :stop - start] = jnp.where(
                    mask, all_keys[:, start:stop].astype(F32), 0.0).astype(BF16)
                values[pair, spot, :stop - start] = jnp.where(
                    mask, all_values[:, start:stop].astype(F32), 0.0).astype(BF16)

    factor = head_dim ** -0.5 * math.log2(math.e)
    tiles = [None] * (-(-width // LANES))
    for pair, (start, stop, at) in enumerate(places):
        size = stop - start
        scores = lax.dot_general(
            q_ref[:, start:stop], keys[pair, :, :size], (((1,), (1,)), ((), ())),
            preferred_element_type=F32)
        probs, scales = [], []
        for side in range(2):
            part = scores[:, side * spots:(side + 1) * spots]
            top = jnp.max(part, axis=-1, keepdims=True)
            weights = jnp.exp2((part - top) * factor)
            scales.append(1.0 / jnp.sum(weights, axis=-1, keepdims=True))
            probs.append(weights.astype(BF16))
        mixed = jnp.dot(jnp.concatenate(probs, axis=-1), values[pair, :, :size],
                        preferred_element_type=F32)
        lane = lax.broadcasted_iota(jnp.int32, (1, size), 1)
        mixed = mixed * jnp.where(lane < at + head_dim, scales[0], scales[1])
        for tile in range(0, size, LANES):
            piece = mixed[:, tile:tile + LANES]
            index = (start + tile) // LANES
            tiles[index] = piece if tiles[index] is None else tiles[index] + piece
    attended = (jnp.concatenate(tiles, axis=-1) + q_ref[...].astype(F32)).astype(BF16)
    tokens = jnp.concatenate(
        [jnp.transpose(tokens_ref[at]) for at in range(tokens_ref.shape[0])], axis=0)
    residual = (
        tokens.astype(F32)
        + jnp.dot(attended, w_proj_ref[...], preferred_element_type=F32)
    ).astype(BF16)
    renormed = layer_norm(residual.astype(F32), -1).astype(BF16)
    ffn = w_up_ref.shape[1]
    chunk = math.gcd(ffn, 768)
    total = jnp.transpose(residual).astype(F32)
    for start in range(0, ffn, chunk):
        hidden = jnp.dot(renormed, w_up_ref[:, start:start + chunk], preferred_element_type=F32)
        total = total + lax.dot_general(
            w_down_ref[:, start:start + chunk], gelu(hidden).astype(BF16),
            (((1,), (1,)), ((), ())), preferred_element_type=F32)
    total = total.astype(BF16)
    cols = tokens_ref.shape[-1]
    for at in range(tokens_ref.shape[0]):
        out_ref[at] = total[:, at * cols:(at + 1) * cols]


def finish(query, tokens, pooled, w_proj, w_up, w_down):
    count, width = query.shape
    spots = pooled.shape[0]
    cols = tokens.shape[-1]
    lines = math.gcd(count // cols, 2 if spots <= 512 else 1)
    block = pl.BlockSpec((lines * cols, width), lambda i: (i, 0))
    turned = pl.BlockSpec((lines, width, cols), lambda i: (i, 0, 0))
    vmem = pl.BlockSpec(memory_space=pltpu.VMEM)
    places = windows(width, HEADS)
    size = max(stop - start for start, stop, _ in places)
    ffn = w_up.shape[1]
    return pl.pallas_call(
        functools.partial(finish_kernel, HEADS),
        grid=(count // cols // lines,),
        out_shape=jax.ShapeDtypeStruct(tokens.shape, BF16),
        in_specs=[block, turned, vmem, vmem, vmem, vmem],
        out_specs=turned,
        scratch_shapes=[
            pltpu.VMEM((len(places), 2 * spots, size), BF16),
            pltpu.VMEM((len(places), 2 * spots, size), BF16),
        ],
        compiler_params=pltpu.CompilerParams(vmem_limit_bytes=(24 if spots <= 512 else 52) * 2**20),
        cost_estimate=pl.CostEstimate(
            flops=2 * count * width * (width + 2 * ffn + 2 * spots),
            bytes_accessed=10 * 2**20, transcendentals=count * (ffn + HEADS * spots)),
        name="finish",
    )(query, tokens, pooled, w_proj, w_up, w_down)


def per_device(rows_n, cols_n, tokens, w_qkv, pool_kernel, key_gain, value_gain, w_proj, w_up,
               w_down):
    turned = jnp.swapaxes(tokens, 1, 2)
    query, pooled = pooled_keys(
        turned, w_qkv, jnp.transpose(pool_kernel, (1, 2, 0, 3)), key_gain, value_gain,
        rows_n, cols_n)
    result = finish(query, turned, pooled.reshape(-1, pooled.shape[-1]), w_proj, w_up, w_down.T)
    return jnp.swapaxes(result, 1, 2)


def solution(mesh):
    in_specs = (P(("maps", "row"), "col", None), P(), P(), P(), P(), P(), P(), P())
    out_specs = P(("maps", "row"), "col", None)
    body = functools.partial(per_device, mesh.shape["row"], mesh.shape["col"])
    return jax.shard_map(
        body, mesh=mesh, in_specs=in_specs, out_specs=out_specs, check_vma=False
    )
```

```python
import functools
import math

import jax
import jax.numpy as jnp
from jax import lax
from jax.experimental import pallas as pl
from jax.experimental.pallas import tpu as pltpu
from jax.sharding import PartitionSpec as P

HEADS = 8
STRIDE = 8
EPS = 1e-06
LANES = 128
MESH = pl.DeviceIdType.MESH
F32 = jnp.float32
BF16 = jnp.bfloat16


def layer_norm(values, axis):
    mean = jnp.mean(values, axis=axis, keepdims=True)
    centred = values - mean
    spread = jnp.mean(centred * centred, axis=axis, keepdims=True)
    return centred * lax.rsqrt(spread + EPS)


def spread_matrix(head_dim, width, heads, shift, dtype):
    feature = lax.broadcasted_iota(jnp.int32, (head_dim, width), 0)
    lane = lax.broadcasted_iota(jnp.int32, (head_dim, width), 1) - shift
    hit = lane == feature
    for head in range(1, heads):
        hit = hit | (lane == feature + head * head_dim)
    return jnp.where(hit, 1.0, 0.0).astype(dtype)


def pooled_keys_kernel(
    rows_n, cols_n, heads,
    tokens_hbm, w_hbm, pool_ref, key_gain_hbm, value_gain_hbm,
    q_hbm, gathered_ref,
    q_ref, q_sem, tokens_ref, w_ref, key_gain_ref, value_gain_ref, load_sem,
    normed, keyval, taps, own, blocks,
    down_out, down_in, diag_out, diag_in, right_out, right_in,
    halo_send, halo_recv, send_sem, recv_sem,
):
    _, width, cols = tokens_ref.shape
    head_dim = width // heads
    groups = cols // STRIDE
    span = pool_ref.shape[0]
    reach = span // 2
    aligned = width // LANES * LANES
    shift = width - aligned
    wide = shift + 2 * width
    row, col = lax.axis_index("row"), lax.axis_index("col")
    has_up, has_down = row > 0, row < rows_n - 1
    has_left, has_right = col > 0, col < cols_n - 1
    to_diag = jnp.logical_and(has_down, has_right)
    from_diag = jnp.logical_and(has_up, has_left)

    loads = []
    for source, target, place in (
        (tokens_hbm, tokens_ref, (pl.ds(reach, STRIDE - reach),)),
        (w_hbm, w_ref, (slice(None), pl.ds(aligned, wide))),
        (tokens_hbm, tokens_ref, (pl.ds(0, reach),)),
        (w_hbm, w_ref, (slice(None), pl.ds(0, aligned))),
        (key_gain_hbm, key_gain_ref, (slice(None),)),
        (value_gain_hbm, value_gain_ref, (slice(None),)),
    ):
        loads.append(pltpu.make_async_copy(
            source.at[place], target.at[place], load_sem.at[len(loads)]))
        loads[-1].start()

    barrier = pltpu.get_barrier_semaphore()
    for step in range(1, rows_n):
        pl.semaphore_signal(
            barrier, inc=1, device_id={"row": lax.rem(row + step, rows_n)}, device_id_type=MESH)
    for step in range(1, cols_n):
        pl.semaphore_signal(
            barrier, inc=1, device_id={"col": lax.rem(col + step, cols_n)}, device_id_type=MESH)

    @pl.when(to_diag)
    def _():
        pl.semaphore_signal(
            barrier, inc=1, device_id={"row": row + 1, "col": col + 1}, device_id_type=MESH)

    @pl.when(from_diag)
    def _():
        pl.semaphore_signal(
            barrier, inc=1, device_id={"row": row - 1, "col": col - 1}, device_id_type=MESH)

    key_spread = spread_matrix(head_dim, shift + width, heads, shift, BF16)
    value_spread = spread_matrix(head_dim, width, heads, 0, BF16)
    def spread_taps(side, matrix):
        room = jnp.zeros((16 - span, head_dim), F32)
        lines = []
        for a in range(span):
            lines += [pool_ref[a].astype(F32)[:, side, :], room]
        lines = jnp.concatenate(lines, axis=0).astype(BF16)
        return jnp.dot(lines, matrix, preferred_element_type=F32)

    spread = jnp.concatenate([spread_taps(0, key_spread), spread_taps(1, value_spread)], axis=-1)
    for a in range(span):
        line = spread[16 * a:16 * a + span]
        below = jnp.zeros((STRIDE - reach - 1, wide), F32)
        above = jnp.zeros((STRIDE - reach, wide), F32)
        taps[0, a] = jnp.concatenate([line[reach:], below], axis=0)
        taps[1, a] = jnp.concatenate([above, line[:reach]], axis=0)

    def project(first, last):
        for at in range(first, last):
            line = pl.ds(at * cols, cols)
            normed[line, :] = jnp.transpose(
                layer_norm(tokens_ref[at].astype(F32), 0).astype(BF16))
        part = pl.ds(first * cols, (last - first) * cols)
        keyval[part, :] = jnp.dot(
            normed[part, :], w_ref[:, aligned:], preferred_element_type=F32).astype(BF16)

    def pool(first, last, offset, here, beyond):
        for start in range(0, wide, LANES):
            lanes = slice(start, min(start + LANES, wide))
            low, high = None, None
            for at in range(first, last):
                values = keyval[at * cols:(at + 1) * cols, lanes].astype(F32)
                values = values.reshape(groups, STRIDE, values.shape[-1])
                one = values * taps[0, at + offset, :, lanes][None]
                two = values * taps[1, at + offset, :, lanes][None]
                low = one if low is None else low + one
                high = two if high is None else high + two
            moved = jnp.concatenate([jnp.zeros_like(high[:1]), high[:-1]], axis=0)
            here[:, lanes] = jnp.sum(low + moved, axis=1)
            beyond[:, lanes] = jnp.sum(high[-1], axis=0, keepdims=True)

    def halo(at, source, target, device):
        return pltpu.make_async_remote_copy(
            src_ref=source, dst_ref=target, send_sem=halo_send.at[at], recv_sem=halo_recv.at[at],
            device_id=device, device_id_type=MESH)

    down = halo(0, down_out, down_in, {"row": lax.rem(row + 1, rows_n)})
    diag = halo(1, diag_out, diag_in,
                {"row": lax.rem(row + 1, rows_n), "col": lax.rem(col + 1, cols_n)})
    right = halo(2, right_out, right_in, {"col": lax.rem(col + 1, cols_n)})

    loads[0].wait()
    loads[1].wait()
    project(reach, STRIDE)
    pool(reach, STRIDE, -reach, down_out, diag_out)
    pl.semaphore_wait(
        barrier, rows_n - 1 + cols_n - 1 + to_diag.astype(jnp.int32) + from_diag.astype(jnp.int32))
    pl.when(has_down)(down.start)
    pl.when(to_diag)(diag.start)
    loads[2].wait()
    project(0, reach)
    pool(0, reach + 1, reach, own, right_out)
    pl.when(has_right)(right.start)

    loads[3].wait()
    q_ref[:, :aligned] = jnp.dot(
        normed[...], w_ref[:, :aligned], preferred_element_type=F32).astype(BF16)
    q_ref[:, aligned:] = keyval[:, :shift]
    q_store = pltpu.make_async_copy(q_ref, q_hbm, q_sem)
    q_store.start()

    @pl.when(jnp.logical_not(has_up))
    def _():
        down_in[...] = jnp.zeros_like(down_in)

    @pl.when(jnp.logical_not(from_diag))
    def _():
        diag_in[...] = jnp.zeros_like(diag_in)

    @pl.when(jnp.logical_not(has_left))
    def _():
        right_in[...] = jnp.zeros_like(right_in)

    pl.when(has_up)(down.wait_recv)
    pl.when(from_diag)(diag.wait_recv)
    pl.when(has_left)(right.wait_recv)

    total = own[...] + down_in[...]
    first_row = lax.broadcasted_iota(jnp.int32, total.shape, 0) == 0
    total = total + jnp.where(first_row, right_in[...] + diag_in[...], 0.0)
    lane = lax.broadcasted_iota(jnp.int32, (1, wide), 1) - shift
    masks = [
        (lane >= at * head_dim) & (lane < (at + 1) * head_dim) for at in range(2 * heads)
    ]

    def head_mean(values):
        result = jnp.zeros_like(values)
        for mask in masks:
            mean = jnp.sum(jnp.where(mask, values, 0.0), axis=-1, keepdims=True) / head_dim
            result = jnp.where(mask, mean, result)
        return result

    def spread_gain(gain_ref, matrix):
        gain = jnp.broadcast_to(gain_ref[...], (8, head_dim))
        return jnp.dot(gain, matrix.astype(F32), precision=lax.Precision.HIGHEST,
                       preferred_element_type=F32)[:1]

    loads[4].wait()
    loads[5].wait()
    gains = jnp.concatenate(
        [spread_gain(key_gain_ref, key_spread), spread_gain(value_gain_ref, value_spread)], axis=-1)
    centred = total - head_mean(total)
    scaled = centred * lax.rsqrt(head_mean(centred * centred) + EPS) * gains
    me = row * cols_n + col
    blocks[me] = scaled[:, shift:].astype(BF16)

    sends = []

    def send(block, device):
        copy = pltpu.make_async_remote_copy(
            src_ref=blocks.at[block], dst_ref=blocks.at[block],
            send_sem=send_sem.at[len(sends)], recv_sem=recv_sem.at[block],
            device_id=device, device_id_type=MESH)
        copy.start()
        sends.append(copy)

    def arrive(block):
        pltpu.make_async_remote_copy(
            src_ref=blocks.at[block], dst_ref=blocks.at[block],
            send_sem=send_sem.at[0], recv_sem=recv_sem.at[block],
            device_id={"col": lax.rem(col + 1, cols_n)}, device_id_type=MESH).wait_recv()

    def flipped(bit):
        return col + bit - 2 * bit * lax.rem(col // bit, 2)

    bits = []
    bit = cols_n // 2
    while bit >= 1:
        bits.append(bit)
        bit //= 2
    order = [0]
    for step in range(1, rows_n // 2 + 1):
        order += [step] if 2 * step == rows_n else [step, rows_n - step]
    for step in reversed(order[1:]):
        send(me, {"row": lax.rem(row + step, rows_n)})
    have = [col]
    for level in range(len(bits) + 1):
        fresh = have if level == 0 else have[len(have) // 2:]
        for at in fresh:
            for step in order:
                block = lax.rem(row + step, rows_n) * cols_n + at
                if not (level == 0 and step == 0):
                    arrive(block)
                for bit in bits[level:]:
                    send(block, {"col": flipped(bit)})
        if level < len(bits):
            bit = bits[level]
            have = have + [at + bit - 2 * bit * lax.rem(at // bit, 2) for at in have]
    gathered_ref[...] = blocks[...]
    q_store.wait()
    for copy in sends:
        copy.wait_send()
    pl.when(has_down)(down.wait_send)
    pl.when(to_diag)(diag.wait_send)
    pl.when(has_right)(right.wait_send)


def pooled_keys(tokens, w_qkv, pool_kernel, key_gain, value_gain, rows_n, cols_n):
    rows, width, cols = tokens.shape
    count = rows * cols
    groups = cols // STRIDE
    span = pool_kernel.shape[0]
    shift = width % LANES
    wide = shift + 2 * width
    spaces = rows_n * cols_n
    sends = rows_n - 1 + rows_n * (cols_n - 1)
    vmem = pl.BlockSpec(memory_space=pltpu.VMEM)
    hbm = pl.BlockSpec(memory_space=pltpu.HBM)
    return pl.pallas_call(
        functools.partial(pooled_keys_kernel, rows_n, cols_n, HEADS),
        out_shape=[
            jax.ShapeDtypeStruct((count, width), BF16),
            jax.ShapeDtypeStruct((spaces, groups, 2 * width), BF16),
        ],
        in_specs=[hbm, hbm, vmem, hbm, hbm],
        out_specs=[hbm, vmem],
        scratch_shapes=[
            pltpu.VMEM((count, width), BF16),
            pltpu.SemaphoreType.DMA,
            pltpu.VMEM(tokens.shape, BF16),
            pltpu.VMEM(w_qkv.shape, BF16),
            pltpu.VMEM((1, key_gain.shape[0]), F32),
            pltpu.VMEM((1, value_gain.shape[0]), F32),
            pltpu.SemaphoreType.DMA((6,)),
            pltpu.VMEM((count, width), BF16),
            pltpu.VMEM((count, wide), BF16),
            pltpu.VMEM((2, span, STRIDE, wide), F32),
            pltpu.VMEM((groups, wide), F32),
            pltpu.VMEM((spaces, groups, 2 * width), BF16),
            pltpu.VMEM((groups, wide), F32),
            pltpu.VMEM((groups, wide), F32),
            pltpu.VMEM((1, wide), F32),
            pltpu.VMEM((1, wide), F32),
            pltpu.VMEM((1, wide), F32),
            pltpu.VMEM((1, wide), F32),
            pltpu.SemaphoreType.DMA((3,)),
            pltpu.SemaphoreType.DMA((3,)),
            pltpu.SemaphoreType.DMA((sends,)),
            pltpu.SemaphoreType.DMA((spaces,)),
        ],
        compiler_params=pltpu.CompilerParams(
            collective_id=0, has_side_effects=True, vmem_limit_bytes=54 * 2**20),
        cost_estimate=pl.CostEstimate(
            flops=2 * count * width * 3 * width, bytes_accessed=6 * 2**20, transcendentals=0),
        name="pooled_keys",
    )(tokens, w_qkv, pool_kernel, key_gain.reshape(1, -1), value_gain.reshape(1, -1))


def windows(width, heads):
    head_dim = width // heads
    result = []
    for head in range(0, heads, 2):
        start = head * head_dim // LANES * LANES
        stop = min(-(-(head + 2) * head_dim // LANES) * LANES, width)
        result.append((start, stop, head * head_dim - start))
    return result


def gelu(x):
    size = jnp.abs(x)
    t = pl.reciprocal(1.0 + (0.3275911 * 0.5 ** 0.5) * size, approx=False)
    tail = 0.5 * 1.061405429
    for term in (-1.453152027, 1.421413741, -0.284496736, 0.254829592):
        tail = tail * t + 0.5 * term
    tail = tail * t * jnp.exp2(x * x * (-0.5 * math.log2(math.e)))
    return jnp.maximum(x, 0.0) - size * tail


def finish_kernel(heads, q_ref, tokens_ref, pooled_ref, w_proj_ref, w_up_ref, w_down_ref,
                  out_ref, keys, values):
    rows, width = q_ref.shape
    head_dim = width // heads
    spots = pooled_ref.shape[0]
    places = windows(width, heads)

    @pl.when(pl.program_id(0) == 0)
    def _():
        all_keys = pooled_ref[:, :width]
        all_values = pooled_ref[:, width:]
        for pair, (start, stop, at) in enumerate(places):
            lane = lax.broadcasted_iota(jnp.int32, (spots, stop - start), 1)
            for side in range(2):
                first = at + side * head_dim
                mask = (lane >= first) & (lane < first + head_dim)
                spot = pl.ds(side * spots, spots)
                keys[pair, spot, :stop - start] = jnp.where(
                    mask, all_keys[:, start:stop].astype(F32), 0.0).astype(BF16)
                values[pair, spot, :stop - start] = jnp.where(
                    mask, all_values[:, start:stop].astype(F32), 0.0).astype(BF16)

    factor = head_dim ** -0.5 * math.log2(math.e)
    tiles = [None] * (-(-width // LANES))
    for pair, (start, stop, at) in enumerate(places):
        size = stop - start
        scores = lax.dot_general(
            q_ref[:, start:stop], keys[pair, :, :size], (((1,), (1,)), ((), ())),
            preferred_element_type=F32)
        probs, scales = [], []
        for side in range(2):
            part = scores[:, side * spots:(side + 1) * spots]
            top = jnp.max(part, axis=-1, keepdims=True)
            weights = jnp.exp2((part - top) * factor)
            scales.append(1.0 / jnp.sum(weights, axis=-1, keepdims=True))
            probs.append(weights.astype(BF16))
        mixed = jnp.dot(jnp.concatenate(probs, axis=-1), values[pair, :, :size],
                        preferred_element_type=F32)
        lane = lax.broadcasted_iota(jnp.int32, (1, size), 1)
        mixed = mixed * jnp.where(lane < at + head_dim, scales[0], scales[1])
        for tile in range(0, size, LANES):
            piece = mixed[:, tile:tile + LANES]
            index = (start + tile) // LANES
            tiles[index] = piece if tiles[index] is None else tiles[index] + piece
    attended = (jnp.concatenate(tiles, axis=-1) + q_ref[...].astype(F32)).astype(BF16)
    tokens = jnp.concatenate(
        [jnp.transpose(tokens_ref[at]) for at in range(tokens_ref.shape[0])], axis=0)
    residual = (
        tokens.astype(F32)
        + jnp.dot(attended, w_proj_ref[...], preferred_element_type=F32)
    ).astype(BF16)
    renormed = layer_norm(residual.astype(F32), -1).astype(BF16)
    ffn = w_up_ref.shape[1]
    chunk = math.gcd(ffn, 768)
    total = jnp.transpose(residual).astype(F32)
    for start in range(0, ffn, chunk):
        hidden = jnp.dot(renormed, w_up_ref[:, start:start + chunk], preferred_element_type=F32)
        total = total + lax.dot_general(
            w_down_ref[:, start:start + chunk], gelu(hidden).astype(BF16),
            (((1,), (1,)), ((), ())), preferred_element_type=F32)
    total = total.astype(BF16)
    cols = tokens_ref.shape[-1]
    for at in range(tokens_ref.shape[0]):
        out_ref[at] = total[:, at * cols:(at + 1) * cols]


def finish(query, tokens, pooled, w_proj, w_up, w_down):
    count, width = query.shape
    spots = pooled.shape[0]
    cols = tokens.shape[-1]
    lines = math.gcd(count // cols, 4 if spots <= 512 else 1)
    block = pl.BlockSpec((lines * cols, width), lambda i: (i, 0))
    turned = pl.BlockSpec((lines, width, cols), lambda i: (i, 0, 0))
    vmem = pl.BlockSpec(memory_space=pltpu.VMEM)
    places = windows(width, HEADS)
    size = max(stop - start for start, stop, _ in places)
    ffn = w_up.shape[1]
    return pl.pallas_call(
        functools.partial(finish_kernel, HEADS),
        grid=(count // cols // lines,),
        out_shape=jax.ShapeDtypeStruct(tokens.shape, BF16),
        in_specs=[block, turned, vmem, vmem, vmem, vmem],
        out_specs=turned,
        scratch_shapes=[
            pltpu.VMEM((len(places), 2 * spots, size), BF16),
            pltpu.VMEM((len(places), 2 * spots, size), BF16),
        ],
        compiler_params=pltpu.CompilerParams(vmem_limit_bytes=(32 if spots <= 512 else 52) * 2**20),
        cost_estimate=pl.CostEstimate(
            flops=2 * count * width * (width + 2 * ffn + 2 * spots),
            bytes_accessed=10 * 2**20, transcendentals=count * (ffn + HEADS * spots)),
        name="finish",
    )(query, tokens, pooled, w_proj, w_up, w_down)


def per_device(rows_n, cols_n, tokens, w_qkv, pool_kernel, key_gain, value_gain, w_proj, w_up,
               w_down):
    turned = jnp.swapaxes(tokens, 1, 2)
    query, pooled = pooled_keys(
        turned, w_qkv, jnp.transpose(pool_kernel, (1, 2, 0, 3)), key_gain, value_gain,
        rows_n, cols_n)
    result = finish(query, turned, pooled.reshape(-1, pooled.shape[-1]), w_proj, w_up, w_down.T)
    return jnp.swapaxes(result, 1, 2)


def solution(mesh):
    in_specs = (P(("maps", "row"), "col", None), P(), P(), P(), P(), P(), P(), P())
    out_specs = P(("maps", "row"), "col", None)
    body = functools.partial(per_device, mesh.shape["row"], mesh.shape["col"])
    return jax.shard_map(
        body, mesh=mesh, in_specs=in_specs, out_specs=out_specs, check_vma=False
    )
```
